128 devices in a mesh: hid: 16 (over x, z), wid: 8 (over y, core).
Axes of the slice: x: 4, y: 4, z: 4, core: 2. Of those that a mesh axis runs over, the one named last changes fastest.
Arguments:
- tokens: bfloat16 [1024, 8192], P(None, 'wid'), may hold values from -6 to 6
- gate_weight: bfloat16 [8192, 28672], P('wid', 'hid'), may hold values from -0.0625 to 0.0625
- up_weight: bfloat16 [8192, 28672], P('wid', 'hid'), may hold values from -0.0625 to 0.0625
- down_weight: bfloat16 [28672, 8192], P('hid', 'wid'), may hold values from -0.03125 to 0.03125
- adapter_id: int32 [1024, 1], replicated, may hold values from 0 to 255; in each aligned block of 1024 rows (0 to 1023, 1024 to 2047, ...) at most 8 rows name the same one
- owner_slot: int32 [256], replicated, may hold values from 0 to 255, each once
- adapt_down: bfloat16 [256, 28672, 64], P(('hid', 'wid')), may hold values from -0.03125 to 0.03125
- adapt_up: bfloat16 [256, 64, 8192], P(('hid', 'wid')), may hold values from -0.75 to 0.75
Outputs:
- mixed: bfloat16 [1024, 8192], P('hid', 'wid')
The draws below stay inside these ranges and needn't reach their ends.
Inputs may be any that keep to these rules, and one draw needn't show every extreme that they name: `adapter_id`: every adapter is named by at least one row and by at most 8 rows; some adapter is named by exactly 8 rows. `owner_slot`: each slot is given to exactly one adapter.
All inputs are finite; a program needn't handle non-finite values.
Results may differ from the reference program's by a relative error of at most 0.006.
Values may be sent and summed in bfloat16 or wider, within the bound.
No kernel may reach another device: no remote copies, remote signals or barrier semaphores. Data moves between devices by JAX's collectives and lax.ppermute only.
A program may use at most 128 MiB of HBM per device.

```python
import math
import jax
import jax.numpy as jnp
import numpy as np
from jax import lax

D = 8192
FF = 28672
RANK = 64
ROWS = 1024
ADAPTERS = 256
CAP = 8


def block_scale(key, extent, pieces, smallest, largest):
    factor_of = 1.0
    for position, parts in pieces:
        draws = jax.random.uniform(jax.random.fold_in(jax.random.fold_in(key, 6), position), (parts,), jnp.float32, smallest / len(pieces), largest / len(pieces))
        factor_of = factor_of * jnp.repeat(jnp.exp(draws), extent[position] // parts).reshape((-1,) + (1,) * (len(extent) - 1 - position))
    return factor_of


def assign_block(rng, own, number, rows, amount, top, most, skew):
    order = jax.random.permutation(rng, amount)
    packed, usual = shares(amount, rows * top, most, skew, True), shares(amount, rows * top, most, skew, False)
    places = jnp.arange(amount)

    def named(lengths, turn):
        used = int((lengths > 0).sum())
        fixed = max(1, used // 4)
        shifted = fixed + (places - fixed + turn * (used - fixed)) % max(1, amount - fixed)
        return jnp.zeros((amount,), jnp.int32).at[order[jnp.where(places < fixed, places, shifted)]].set(jnp.asarray(lengths, jnp.int32))

    lengths = jnp.where(number % 4 == 0, named(packed, number // 4), named(usual, number - number // 4 - 1))
    mixed = jax.random.permutation(jax.random.fold_in(own, 3), amount)
    giver, sink = mixed[0:amount // 2 * 2:2], mixed[1:amount // 2 * 2:2]
    slack = jnp.minimum(lengths[giver] - 1, most - lengths[sink]) // 2
    slack = jnp.where((giver == order[0]) | (sink == order[0]) | (lengths[sink] == 0), 0, jnp.maximum(slack, 0))
    shifted = jax.random.randint(jax.random.fold_in(own, 4), (amount // 2,), 0, 1 << 20) % (slack + 1)
    lengths = lengths.at[giver].add(-shifted).at[sink].add(shifted)
    items = jnp.searchsorted(jnp.cumsum(lengths), jnp.arange(rows * top), side="right").astype(jnp.int32)
    table = items.reshape(top, rows).T
    table = table[jax.random.permutation(jax.random.fold_in(own, 1), rows)]
    turn = jax.random.randint(jax.random.fold_in(own, 2), (rows, 1), 0, top)
    return jnp.take_along_axis(table, (jnp.arange(top)[None, :] + turn) % top, axis=1)


def shares(amount, total, most, lean, full):
    weights = [(1 << 20) // math.isqrt(rank ** lean) + 1 for rank in range(1, amount + 1)]
    largest = most if full else min(most, max(-(-total // amount), total * weights[0] // sum(weights)))
    least = 1 if total - largest >= amount - 1 else 0
    holding, spare = [largest] + [least] * (amount - 1), total - largest - least * (amount - 1)
    while spare > 0:
        candidates = [i for i in range(1, amount) if holding[i] < largest] or [i for i in range(1, amount) if holding[i] < most]
        pool, budget = sum([weights[i] for i in candidates]), spare
        for i in candidates:
            addition = min(most - holding[i], max(1, budget * weights[i] // pool), spare)
            holding[i] = holding[i] + addition
            spare = spare - addition
    return np.array(holding)


def centred(rng, extent, width, bound, pieces=(), kind=jnp.bfloat16):
    array = jax.random.normal(rng, extent, jnp.float32) * width
    if len(pieces) > 0:
        array = block_scale(rng, extent, pieces, -0.22, 0.18) * array
    return jnp.clip(array, min=-bound, max=bound).astype(kind)


def setup_inputs(seed: int = 0) -> dict:
    streams_of = jax.random.split(jax.random.key(seed), 9)
    tokens = centred(streams_of[0], (ROWS, D), 1.0, 6.0, ((1, 8),))
    gate_weight = centred(streams_of[1], (D, FF), D ** -0.5, 0.0625, ((0, 8), (1, 16)))
    up_weight = centred(streams_of[2], (D, FF), D ** -0.5, 0.0625, ((0, 8), (1, 16)))
    down_weight = centred(streams_of[3], (FF, D), FF ** -0.5, 0.03125, ((0, 16), (1, 8)))
    adapter_id_keys = jax.random.split(jax.random.fold_in(streams_of[4], 1), ROWS // ROWS)
    adapter_id_turns = jax.random.permutation(jax.random.fold_in(streams_of[4], 3), ROWS // ROWS)
    adapter_id = jax.vmap(lambda own, number: assign_block(jax.random.fold_in(streams_of[4], 2), own, number, ROWS, ADAPTERS, 1, CAP, 2))(adapter_id_keys, adapter_id_turns).reshape((ROWS, 1))
    owner_slot = jax.random.permutation(streams_of[5], ADAPTERS).astype(jnp.int32)
    adapt_down = centred(streams_of[6], (ADAPTERS, FF, RANK), FF ** -0.5, 0.03125, ((0, 128),))
    adapt_up = centred(streams_of[7], (ADAPTERS, RANK, D), RANK ** -0.5, 0.75, ((0, 128),))
    return {"tokens": tokens, "gate_weight": gate_weight, "up_weight": up_weight, "down_weight": down_weight, "adapter_id": adapter_id, "owner_slot": owner_slot, "adapt_down": adapt_down, "adapt_up": adapt_up}


def reference(tokens, gate_weight, up_weight, down_weight, adapter_id, owner_slot, adapt_down, adapt_up):
    gate = jnp.dot(tokens, gate_weight, preferred_element_type=jnp.float32)
    up_value = jnp.dot(tokens, up_weight, preferred_element_type=jnp.float32)
    hidden = (jax.nn.silu(gate) * up_value).astype(jnp.bfloat16)
    row_slot = owner_slot[adapter_id[:, 0]].astype(jnp.int32)

    def one_row(item):
        values, slot_id = item
        low_rank = jnp.dot(values[None, :], adapt_down[slot_id], preferred_element_type=jnp.float32).astype(jnp.bfloat16)
        return jnp.dot(low_rank, adapt_up[slot_id], preferred_element_type=jnp.float32).astype(jnp.bfloat16)[0]

    adapted = lax.map(one_row, (hidden, row_slot))
    base = jnp.dot(hidden, down_weight, preferred_element_type=jnp.float32)
    return (base + adapted.astype(jnp.float32)).astype(jnp.bfloat16)
```

```python
import jax
import jax.numpy as jnp
from jax import lax
from jax.sharding import Mesh, PartitionSpec as P

BF = jnp.bfloat16
F32 = jnp.float32
CHUNKS = (1024, 768)
ORDER = (0, 1, 3, 2)
STREAMS = (((0, 1, 2, 3), (2, 3, 0, 1)), ((1, 0, 3, 2), (3, 2, 1, 0)))


def gray(v):
    return v ^ (v >> 1)


def flip_a(v):
    return v ^ 1


def flip_b(v):
    return 3 - v


def hid_perm(dims):
    pairs = []
    for x in range(4):
        for z in range(4):
            for k in range(2):
                move = flip_b if dims[k] % 2 == 0 else flip_a
                to = (move(x), z) if dims[k] < 2 else (x, move(z))
                pairs.append(((x * 4 + z) * 2 + k, (to[0] * 4 + to[1]) * 2 + k))
    return pairs


def part(array, index, rows):
    return lax.dynamic_slice_in_dim(array, index * rows, rows, 0)


def join(bit, mine, other):
    return jnp.where(
        bit == 0, jnp.concatenate([mine, other], 0), jnp.concatenate([other, mine], 0)
    )


def per_device(
    tokens, gate_weight, up_weight, down_weight, adapter_id, owner_slot, adapt_down, adapt_up
):
    x, z, y, c = (lax.axis_index(n) for n in ("x", "z", "y", "c"))
    row_count = tokens.shape[0]
    ff_local = gate_weight.shape[1]
    d_local = down_weight.shape[1]
    adapter_count = owner_slot.shape[0]
    per_dev = adapt_down.shape[0]
    capacity = 2 * row_count // adapter_count
    wid_axes, hid_axes = ("y", "c"), ("x", "z")
    wid_index, hid_index = y * 2 + c, x * 4 + z
    block = row_count // 16

    gray_y = gray(y)
    low_y, high_y = gray_y & 1, gray_y >> 1
    keep1 = jnp.where(c == 0, low_y, high_y)
    keep2 = jnp.where(c == 0, high_y, low_y)
    swap_perm = [(i, i ^ 1) for i in range(8)]
    first = (flip_a, flip_b)
    perm1 = [(v * 2 + k, first[k](v) * 2 + k) for v in range(4) for k in range(2)]
    perm2 = [(v * 2 + k, first[1 - k](v) * 2 + k) for v in range(4) for k in range(2)]

    blocks = [(ORDER[i], ORDER[j]) for i in range(4) for j in range(4)]
    order = [bx * 4 + bz for bx, bz in blocks]
    permuted = jnp.concatenate([tokens[b * block : (b + 1) * block] for b in order], 0)
    row_id = (
        jnp.asarray(order, jnp.int32)[:, None] * block + jnp.arange(block, dtype=jnp.int32)
    ).reshape(-1)

    half = row_count // 2
    away = part(permuted, 1 - c, half)
    home = part(permuted, c, half)

    row_adapter = adapter_id[:, 0]
    adapter_range = jnp.arange(adapter_count, dtype=jnp.int32)
    row_slot = jnp.sum(
        jnp.where(row_adapter[:, None] == adapter_range[None, :], owner_slot[None, :], 0), axis=1
    )
    positions = jnp.arange(row_count, dtype=jnp.int32)
    earlier = (row_adapter[:, None] == row_adapter[None, :]) & (
        positions[None, :] < positions[:, None]
    )
    row_rank = jnp.sum(earlier.astype(jnp.int32), axis=1)

    def regroup(v):
        return jnp.concatenate([v[b * block : (b + 1) * block] for b in order], 0)

    row_slot, row_rank = regroup(row_slot), regroup(row_rank)
    row_owner = row_slot // per_dev
    row_local = row_slot % per_dev
    owner_hid = row_owner // 8
    owner_wid = row_owner % 8
    send_index = jnp.where(
        owner_wid == wid_index, (owner_hid * per_dev + row_local) * capacity + row_rank, -1
    )
    send_slots = jnp.arange(16 * per_dev * capacity, dtype=jnp.int32)
    selector = (send_slots[:, None] == send_index[None, :]).astype(BF)
    landing_index = jnp.where(
        owner_hid == hid_index, (owner_wid * per_dev + row_local) * capacity + row_rank, -1
    )
    landing_slots = jnp.arange(8 * per_dev * capacity, dtype=jnp.int32)
    landing = (landing_index[:, None] == landing_slots[None, :]).astype(BF)

    def dot(a, b):
        return jnp.dot(a, b, preferred_element_type=F32)

    low_rank = 0.0
    result = 0.0
    down_by_hid = adapt_down.reshape(per_dev, 16, ff_local, adapt_down.shape[2])
    offset = 0
    for width in CHUNKS:
        columns = slice(offset, offset + width)
        offset += width
        gw, uw = gate_weight[:, columns], up_weight[:, columns]
        far = [lax.ppermute(dot(away, w).astype(BF), wid_axes, swap_perm) for w in (gw, uw)]
        near = [dot(home, w) for w in (gw, uw)]
        sums = jnp.stack([n + f.astype(F32) for n, f in zip(near, far)], 1)
        for perm, keep, rows in ((perm1, keep1, half // 2), (perm2, keep2, half // 4)):
            arrived = lax.ppermute(part(sums, 1 - keep, rows).astype(BF), wid_axes, perm)
            sums = part(sums, keep, rows) + arrived.astype(F32)
        hidden = (jax.nn.silu(sums[:, 0]) * sums[:, 1]).astype(BF)
        hidden = join(keep2, hidden, lax.ppermute(hidden, wid_axes, perm2))
        hidden = join(keep1, hidden, lax.ppermute(hidden, wid_axes, perm1))
        hidden = join(c, hidden, lax.ppermute(hidden, wid_axes, swap_perm))
        packed = dot(selector, hidden).astype(BF).reshape(16, per_dev, capacity, width)
        arrived = lax.all_to_all(packed, hid_axes, split_axis=0, concat_axis=0, tiled=True)
        low_rank = low_rank + jnp.einsum(
            "hjcf,jhfr->jcr", arrived, down_by_hid[:, :, columns], preferred_element_type=F32
        )
        result = result + dot(hidden, down_weight[columns])
    adapted = jnp.einsum(
        "jcr,jrd->jcd", low_rank.astype(BF), adapt_up, preferred_element_type=F32
    ).astype(BF)
    slots = per_dev * capacity
    adapted = adapted.reshape(slots, 8, d_local).transpose(1, 0, 2)
    returned = lax.all_to_all(adapted, wid_axes, split_axis=0, concat_axis=0, tiled=True)
    result = result + dot(landing, returned.reshape(8 * slots, d_local))

    gray_x, gray_z = gray(x), gray(z)
    bits = (gray_x >> 1, gray_x & 1, gray_z >> 1, gray_z & 1)
    width = d_local // 2
    outs = []
    for stream, dims in enumerate(STREAMS):
        value = result[:, stream * width : (stream + 1) * width].reshape(16, block, width)
        left = [[0, 1, 2, 3], [0, 1, 2, 3]]
        for step in range(4):
            at = [left[k].index(dims[k][step]) for k in range(2)]
            bit = jnp.where(c == 0, bits[dims[0][step]], bits[dims[1][step]])
            count = value.shape[0]

            def pick(value, bit):
                both = []
                for k in range(2):
                    shaped = value.reshape(2 ** at[k], 2, -1, block, width)
                    taken = lax.dynamic_index_in_dim(shaped, bit, 1, keepdims=False)
                    both.append(taken.reshape(count // 2, block, width))
                return both[0] if at[0] == at[1] else jnp.where(c == 0, both[0], both[1])

            sent = pick(value, 1 - bit).astype(BF)
            arrived = lax.ppermute(sent, ("x", "z", "c"), hid_perm([dims[k][step] for k in range(2)]))
            value = pick(value, bit) + arrived.astype(F32)
            for k in range(2):
                left[k].remove(dims[k][step])
        outs.append(value[0])
    return jnp.concatenate(outs, 1).astype(BF)


def solution(mesh):
    fine = Mesh(mesh.devices.reshape(4, 4, 4, 2), ("x", "z", "y", "c"))
    hid, wid = ("x", "z"), ("y", "c")
    return jax.shard_map(
        per_device,
        mesh=fine,
        in_specs=(
            P(None, wid),
            P(wid, hid),
            P(wid, hid),
            P(hid, wid),
            P(),
            P(),
            P(hid + wid, None, None),
            P(hid + wid, None, None),
        ),
        out_specs=P(hid, wid),
        check_vma=False,
    )
```

```python
import jax
import jax.numpy as jnp
from jax import lax
from jax.experimental import pallas as pl
from jax.experimental.pallas import tpu as pltpu
from jax.sharding import Mesh, PartitionSpec as P

BF = jnp.bfloat16
F32 = jnp.float32
TILE = 256
STEP_TYPES = (BF, BF, BF, F32)
VM_OWN, VM_LOW = 24, 24
STREAMS = (((0, 1, 2, 3), (2, 3, 0, 1)), ((1, 0, 3, 2), (3, 2, 1, 0)))


def flip_a(v):
    return v ^ 1


def flip_b(v):
    return 3 - v


def gray(v):
    return v ^ (v >> 1)


def hid_perm(dims):
    pairs = []
    for x in range(4):
        for z in range(4):
            for k in range(2):
                move = flip_b if dims[k] % 2 == 0 else flip_a
                to = (move(x), z) if dims[k] < 2 else (x, move(z))
                pairs.append(((x * 4 + z) * 2 + k, (to[0] * 4 + to[1]) * 2 + k))
    return pairs


def dot(a, b):
    return jnp.dot(a, b, preferred_element_type=F32)


def take(ref, table, start, count, rows):
    return jnp.concatenate(
        [ref[pl.ds(pl.multiple_of(table[start + p] * rows, rows), rows), :] for p in range(count)], 0
    )


def call(body, grid, ins, outs, mib, flops=0, moved=0, after=(), table=None, scratch=()):
    first = 0 if table is None else 1
    token_spec = pl.BlockSpec((8, 128), lambda *i: (0, 0))

    def kernel(*refs):
        used = refs[: first + len(ins)] + refs[first + len(ins) + len(after) :]
        used[first + len(ins) + len(outs)][...] = jnp.zeros((8, 128), F32)
        body(*used[: first + len(ins) + len(outs)], *used[first + len(ins) + len(outs) + 1 :])

    specs = [spec for _, spec in ins] + [pl.BlockSpec(memory_space=pl.ANY)] * len(after)
    args = [] if table is None else [table]
    args += [v for v, _ in ins] + list(after)
    return pl.pallas_call(
        kernel,
        out_shape=[jax.ShapeDtypeStruct(*o[0]) for o in outs]
        + [jax.ShapeDtypeStruct((8, 128), F32)],
        grid_spec=pltpu.PrefetchScalarGridSpec(
            num_scalar_prefetch=first,
            grid=(grid,),
            in_specs=specs,
            out_specs=[o[1] for o in outs] + [token_spec],
            scratch_shapes=list(scratch),
        ),
        compiler_params=pltpu.CompilerParams(
            vmem_limit_bytes=mib * 2**20, dimension_semantics=("arbitrary",)
        ),
        cost_estimate=pl.CostEstimate(flops=flops, bytes_accessed=moved, transcendentals=0),
    )(*args)


def block_of(*shape):
    return pl.BlockSpec(shape, lambda *_: (0,) * len(shape))


def whole(v):
    return v, pl.BlockSpec(v.shape, lambda *_: (0,) * v.ndim)


def own_sums(table, tokens, weight, after=()):
    rows, depth = tokens.shape
    width = weight.shape[1] // 2

    def body(table, tokens, weight, out):
        left = take(tokens, table, 1, 4, rows // 4)
        for start in range(0, width, TILE):
            at = slice(start, min(start + TILE, width))
            out[:, at] = dot(left, weight[:, at])

    return call(
        body, 1, [whole(tokens), (weight, pl.BlockSpec((depth, width), lambda j, t: (0, t[0])))],
        [(((rows, width), F32), block_of(rows, width))],
        VM_OWN, 2 * rows * depth * width, 2 * depth * width, after, table,
    )


def add_sums(table, tokens, weight, own, after=()):
    rows, depth = tokens.shape
    width = weight.shape[1]
    half = rows // 2

    def body(table, tokens, weight, own, sent, kept):
        left = take(tokens, table, 1, 4, rows // 4)
        for start in range(0, width, TILE):
            at = slice(start, min(start + TILE, width))
            total = dot(left, weight[:, at]) + own[:, at]
            kept[:, at] = total[:half]
            sent[:, at] = total[half:].astype(sent.dtype)

    return call(
        body, 1, [whole(tokens), whole(weight), whole(own)],
        [(((half, width), BF), block_of(half, width)), (((half, width), F32), block_of(half, width))],
        30, 2 * rows * depth * width, 2 * depth * width, after, table,
    )


def add_halves(kept, arrived, after=()):
    rows, width = kept.shape
    half = rows // 2

    def body(kept_in, arrived, sent, kept):
        total = kept_in[...] + arrived[...].astype(F32)
        kept[...] = total[:half]
        sent[...] = total[half:].astype(sent.dtype)

    return call(
        body, 1, [whole(kept), whole(arrived)],
        [(((half, width), BF), block_of(half, width)), (((half, width), F32), block_of(half, width))],
        16, 4 * rows * width, 9 * rows * width, after,
    )


def activate(gate, gate_arrived, up, up_arrived):
    def body(gate, gate_arrived, up, up_arrived, out):
        gates = gate[...] + gate_arrived[...].astype(F32)
        ups = up[...] + up_arrived[...].astype(F32)
        out[...] = (jax.nn.silu(gates) * ups).astype(BF)

    rows, width = gate.shape
    return call(
        body, 1, [whole(v) for v in (gate, gate_arrived, up, up_arrived)],
        [((gate.shape, BF), block_of(rows, width))],
        16, 20 * rows * width, 14 * rows * width,
    )


def pack(table, selectors, mine, theirs):
    slots, rows = selectors[0].shape
    width = mine.shape[1]

    def body(table, first, second, mine, theirs, out):
        for ref, selector, turn in ((mine, first, 0), (theirs, second, 1)):
            value = dot(selector[...], ref[...]).astype(out.dtype)
            for side in range(2):
                @pl.when((table[0] ^ turn) == side)
                def _():
                    out[:, side * width : (side + 1) * width] = value

    return call(
        body, 1, [whole(selectors[0]), whole(selectors[1]), whole(mine), whole(theirs)],
        [(((slots, 2 * width), BF), block_of(slots, 2 * width))],
        20, 4 * slots * rows * width, 4 * rows * width, (), table,
    )


def down(table, weight, mine, theirs, after):
    depth, width = weight.shape
    rows, half = mine.shape

    def body(table, weight, mine, theirs, out):
        side = table[0]
        left = mine[...]
        right = take(theirs, table, 5, 4, rows // 4)
        for start in range(0, width, TILE):
            at = slice(start, start + TILE)
            near = weight[pl.ds(pl.multiple_of(side * half, half), half), at]
            far = weight[pl.ds(pl.multiple_of((1 - side) * half, half), half), at]
            out[:, at] = dot(left, near) + dot(right, far)

    return call(
        body, 1, [whole(weight), whole(mine), whole(theirs)],
        [(((rows, width), F32), block_of(rows, width))],
        36, 2 * rows * depth * width, 2 * rows * depth + 2 * depth * width, after, table,
    )


def adapt(arrived, first, second, per_dev, pieces, after):
    groups, slots, width = arrived.shape
    ranks, columns = second.shape
    piece = columns // pieces

    def body(rows, first, second, out, held, low_ref):
        h = pl.program_id(0)

        @pl.when(h == 0)
        def _():
            low_ref[...] = jnp.zeros_like(low_ref)

        low_ref[...] += lax.dot_general(
            rows[0], first[...], (((1,), (1,)), ((), ())), preferred_element_type=F32
        )

        @pl.when(h == groups - 1)
        def _():
            low = low_ref[...]
            row = lax.broadcasted_iota(jnp.int32, low.shape, 0) // (slots // per_dev)
            column = lax.broadcasted_iota(jnp.int32, low.shape, 1) // (ranks // per_dev)
            own = jnp.where(row == column, low, 0.0).astype(BF)
            for j in range(pieces):
                out[j] = dot(own, second[:, j * piece : (j + 1) * piece]).astype(out.dtype)

    return call(
        lambda rows, first, second, out, low: body(rows, first, second, out, None, low), groups,
        [
            (arrived, pl.BlockSpec((1, slots, width), lambda h: (h, 0, 0))),
            (first, pl.BlockSpec((ranks, width), lambda h: (0, h))),
            whole(second),
        ],
        [(((pieces, slots, piece), BF), block_of(pieces, slots, piece))],
        VM_LOW, 2 * slots * ranks * width * groups, 2 * ranks * width * groups, after, None,
        [pltpu.VMEM((slots, ranks), F32)],
    )


def land(table, base, landing, returned):
    rows, columns = base.shape
    width, slots = columns // 2, returned.shape[0]
    count = 8
    block = rows // 2 // count
    half = pl.BlockSpec((rows // 2, width), lambda s, t: (0, 0))

    def body(table, base, landing, returned, *outs):
        for stream in range(2):
            at = slice(stream * width, (stream + 1) * width)
            for ref, start in ((outs[2 * stream], count), (outs[2 * stream + 1], 0)):
                first = stream * 2 * count + start
                left = take(landing, table, first, count, block)
                near = jnp.concatenate(
                    [
                        base[pl.ds(pl.multiple_of(table[first + p] * block, block), block), at]
                        for p in range(count)
                    ],
                    0,
                )
                ref[...] = (near + dot(left, returned[:, at])).astype(ref.dtype)

    shape = (rows // 2, width)
    outs = [((shape, BF), half), ((shape, F32), half)] * 2
    return call(
        body, 1, [whole(base), whole(landing), whole(returned)], outs,
        20, 2 * rows * slots * columns, 10 * rows * columns, (), table,
    )


def per_device(
    tokens, gate_weight, up_weight, down_weight, adapter_id, owner_slot, adapt_down, adapt_up
):
    x, z, y, c = (lax.axis_index(n) for n in ("x", "z", "y", "c"))
    row_count = tokens.shape[0]
    d_local = down_weight.shape[1]
    adapter_count = owner_slot.shape[0]
    per_dev, ff_count, rank = adapt_down.shape
    capacity = 2 * row_count // adapter_count
    slots = per_dev * capacity
    wid_axes, hid_axes = ("y", "c"), ("x", "z")
    wid_index, hid_index = y * 2 + c, x * 4 + z

    swap_perm = [(i, i ^ 1) for i in range(8)]
    first = (flip_a, flip_b)
    perm1 = [(v * 2 + k, first[k](v) * 2 + k) for v in range(4) for k in range(2)]
    perm2 = [(v * 2 + k, first[1 - k](v) * 2 + k) for v in range(4) for k in range(2)]

    gray_y = gray(y)
    low_y, high_y = gray_y & 1, gray_y >> 1
    four = jnp.arange(4, dtype=jnp.int32)
    ff_half = gate_weight.shape[1] // 2

    def at_place(core):
        one, two = four >> 1, four & 1
        low = jnp.where(core == 0, one, two) ^ low_y
        high = jnp.where(core == 0, two, one) ^ high_y
        return low * 2 + high

    def place_of(core, blocks):
        low, high = (blocks >> 1) ^ low_y, (blocks & 1) ^ high_y
        return jnp.where(core == 0, low * 2 + high, high * 2 + low)

    home_blocks, away_blocks = at_place(c), at_place(1 - c)
    table = jnp.concatenate([c[None], home_blocks, place_of(1 - c, home_blocks)])

    bits = jnp.stack([gray(x) >> 1, gray(x) & 1, gray(z) >> 1, gray(z) & 1])
    sixteen = jnp.arange(16, dtype=jnp.int32)
    land_tables = []
    for dims in STREAMS:
        found = []
        for d in range(4):
            shift = jnp.where(c == 0, 3 - dims[0].index(d), 3 - dims[1].index(d))
            found.append(((sixteen >> shift) & 1) ^ bits[d])
        at_x, at_z = gray(found[0] * 2 + found[1]), gray(found[2] * 2 + found[3])
        land_tables.append(place_of(c, at_x) * 4 + at_z)
    land_table = jnp.concatenate(land_tables)

    def selections(token):
        row_adapter = adapter_id[:, 0] + token[0, 0].astype(jnp.int32)
        adapter_range = jnp.arange(adapter_count, dtype=jnp.int32)
        row_slot = jnp.sum(
            jnp.where(row_adapter[:, None] == adapter_range[None, :], owner_slot[None, :], 0), axis=1
        )
        positions = jnp.arange(row_count, dtype=jnp.int32)
        earlier = (row_adapter[:, None] == row_adapter[None, :]) & (
            positions[None, :] < positions[:, None]
        )
        row_rank = jnp.sum(earlier.astype(jnp.int32), axis=1)
        row_owner = row_slot // per_dev
        owner_hid, owner_wid = row_owner // 8, row_owner % 8
        place = (row_slot % per_dev) * capacity + row_rank

        def own_order(v, blocks):
            chosen = blocks[:, None] == four[None, :]
            v = v.reshape(1, 4, row_count // 4)
            return jnp.sum(jnp.where(chosen[:, :, None], v, 0), axis=1).reshape(-1)

        send_index = jnp.where(owner_wid == wid_index, owner_hid * slots + place, -1)
        send_slots = jnp.arange(16 * slots, dtype=jnp.int32)[:, None]
        selectors = [
            (send_slots == own_order(send_index, blocks)[None, :]).astype(BF)
            for blocks in (home_blocks, away_blocks)
        ]
        land_index = jnp.where(owner_hid == hid_index, owner_wid * slots + place, -1)
        land_index = own_order(land_index, home_blocks)
        landing = (land_index[:, None] == jnp.arange(8 * slots, dtype=jnp.int32)[None, :]).astype(BF)
        return selectors, landing

    down_factor = adapt_down.transpose(0, 2, 1).reshape(per_dev * rank, ff_count)
    up_factor = adapt_up.reshape(per_dev * rank, adapt_up.shape[2])

    swap, one, two = (
        lambda v, perm=perm: lax.ppermute(v, wid_axes, perm) for perm in (swap_perm, perm1, perm2)
    )
    far_tokens = swap(tokens)
    far_gate, far_up = (
        swap(lax.dynamic_slice_in_dim(w, (1 - c) * ff_half, ff_half, 1))
        for w in (gate_weight, up_weight)
    )
    own, token = own_sums(table, tokens, gate_weight)
    sent_gate, kept_gate, token = add_sums(table, far_tokens, far_gate, own, [token])
    own, token = own_sums(table, tokens, up_weight, [token])
    sent_up, kept_up, token = add_sums(table, far_tokens, far_up, own, [token])
    selectors, landing = selections(token)
    order = [token, *selectors, landing]
    sent_gate, kept_gate, token = add_halves(kept_gate, one(sent_gate), order)
    sent_up, kept_up, token = add_halves(kept_up, one(sent_up), [token])
    hidden, _ = activate(kept_gate, two(sent_gate), kept_up, two(sent_up))
    hidden = jnp.concatenate([hidden, two(hidden)], 0)
    mine = jnp.concatenate([hidden, one(hidden)], 0)
    theirs = swap(mine)
    packed, token = pack(table, selectors, mine, theirs)
    packed = packed.reshape(16, slots, packed.shape[1])
    arrived = lax.all_to_all(packed, hid_axes, split_axis=0, concat_axis=0, tiled=True)
    base, token = down(table, down_weight, mine, theirs, [token])
    adapted, _ = adapt(arrived, down_factor, up_factor, per_dev, 8, [token])
    returned = lax.all_to_all(adapted, wid_axes, split_axis=0, concat_axis=0, tiled=True)
    ends = land(land_table, base, landing, returned.reshape(8 * slots, d_local))

    outs = []
    for stream, dims in enumerate(STREAMS):
        value = None
        for step in range(4):
            perm = hid_perm([dims[k][step] for k in range(2)])
            if step == 0:
                going, value = ends[2 * stream], ends[2 * stream + 1]
            else:
                half = value.shape[0] // 2
                going, value = value[half:].astype(STEP_TYPES[step]), value[:half]
            value = value + lax.ppermute(going, ("x", "z", "c"), perm).astype(F32)
        outs.append(value)
    return jnp.concatenate(outs, 1).astype(BF)


def solution(mesh):
    fine = Mesh(mesh.devices.reshape(4, 4, 4, 2), ("x", "z", "y", "c"))
    hid, wid = ("x", "z"), ("y", "c")
    return jax.shard_map(
        per_device,
        mesh=fine,
        in_specs=(
            P(None, wid),
            P(wid, hid),
            P(wid, hid),
            P(hid, wid),
            P(),
            P(),
            P(hid + wid, None, None),
            P(hid + wid, None, None),
        ),
        out_specs=P(hid, wid),
        check_vma=False,
    )
```

```python
import jax
import jax.numpy as jnp
from jax import lax
from jax.experimental import pallas as pl
from jax.experimental.pallas import tpu as pltpu
from jax.sharding import Mesh, PartitionSpec as P

BF = jnp.bfloat16
F32 = jnp.float32
TILE = 256
STEP_TYPES = (BF, BF, BF, F32)
VM_SPLIT, VM_OWN, VM_SUMS, VM_LOW, VM_DOWN, VM_LAND = 20, 20, 20, 16, 20, 16
WIDTHS = (512, 384)
FLOPS = 2 * 10**10
STREAMS = (((0, 1, 2, 3), (2, 3, 0, 1)), ((1, 0, 3, 2), (3, 2, 1, 0)))


def flip_a(v):
    return v ^ 1


def flip_b(v):
    return 3 - v


def gray(v):
    return v ^ (v >> 1)


def hid_perm(dims):
    pairs = []
    for x in range(4):
        for z in range(4):
            for k in range(2):
                move = flip_b if dims[k] % 2 == 0 else flip_a
                to = (move(x), z) if dims[k] < 2 else (x, move(z))
                pairs.append(((x * 4 + z) * 2 + k, (to[0] * 4 + to[1]) * 2 + k))
    return pairs


def dot(a, b):
    return jnp.dot(a, b, preferred_element_type=F32)


def take(ref, table, start, count, rows):
    return jnp.concatenate(
        [ref[pl.ds(pl.multiple_of(table[start + p] * rows, rows), rows), :] for p in range(count)], 0
    )


def call(body, grid, ins, outs, mib, after=(), table=None, flops=1):
    first = 0 if table is None else 1
    token_spec = pl.BlockSpec((8, 128), lambda *i: (0, 0))

    def kernel(*refs):
        used = refs[: first + len(ins)] + refs[first + len(ins) + len(after) :]
        used[first + len(ins) + len(outs)][...] = jnp.zeros((8, 128), F32)
        body(*used[: first + len(ins) + len(outs)], *used[first + len(ins) + len(outs) + 1 :])

    specs = [spec for _, spec in ins] + [pl.BlockSpec(memory_space=pl.ANY)] * len(after)
    args = [] if table is None else [table]
    args += [v for v, _ in ins] + list(after)
    return pl.pallas_call(
        kernel,
        out_shape=[jax.ShapeDtypeStruct(*o[0]) for o in outs]
        + [jax.ShapeDtypeStruct((8, 128), F32)],
        grid_spec=pltpu.PrefetchScalarGridSpec(
            num_scalar_prefetch=first,
            grid=(grid,),
            in_specs=specs,
            out_specs=[o[1] for o in outs] + [token_spec],
        ),
        compiler_params=pltpu.CompilerParams(
            vmem_limit_bytes=mib * 2**20, dimension_semantics=("arbitrary",)
        ),
        cost_estimate=pl.CostEstimate(flops=flops, bytes_accessed=1, transcendentals=0),
    )(*args)


def block_of(*shape):
    return pl.BlockSpec(shape, lambda *_: (0,) * len(shape))


def whole(v):
    return v, pl.BlockSpec(v.shape, lambda *_: (0,) * v.ndim)


def split_columns(table, gate, up, offset, count, after):
    depth = gate.shape[0]
    width = gate.shape[1] // 2

    def body(table, gate, up, out):
        out[0] = gate[:, offset : offset + count]
        out[1] = up[:, offset : offset + count]

    block = pl.BlockSpec((depth, width), lambda j, t: (0, 1 - t[0]))
    return call(
        body, 1, [(gate, block), (up, block)],
        [(((2, depth, count), BF), block_of(2, depth, count))],
        VM_SPLIT, after, table,
    )


def own_sums(table, tokens, gate, up, offset, count, after=()):
    rows, depth = tokens.shape
    width = gate.shape[1] // 2

    def body(table, tokens, gate, up, out):
        left = take(tokens, table, 1, 4, rows // 4)
        for i, weight in enumerate((gate, up)):
            for start in range(0, count, TILE):
                stop = min(start + TILE, count)
                out[i, :, start:stop] = dot(left, weight[:, offset + start : offset + stop])

    block = pl.BlockSpec((depth, width), lambda j, t: (0, t[0]))
    return call(
        body, 1, [whole(tokens), (gate, block), (up, block)],
        [(((2, rows, count), F32), block_of(2, rows, count))],
        VM_OWN, after, table,
    )


def add_sums(table, far_tokens, far, own, after=()):
    rows = far_tokens.shape[0]
    count = far.shape[2]
    half = rows // 2

    def body(table, far_tokens, far, own, sent, kept):
        left = take(far_tokens, table, 1, 4, rows // 4)
        for i in range(2):
            for start in range(0, count, TILE):
                at = slice(start, min(start + TILE, count))
                total = dot(left, far[i, :, at]) + own[i, :, at]
                kept[i, :, at] = total[:half]
                sent[i, :, at] = total[half:].astype(sent.dtype)

    shape = (2, half, count)
    return call(
        body, 1, [whole(far_tokens), whole(far), whole(own)],
        [((shape, BF), block_of(*shape)), ((shape, F32), block_of(*shape))],
        VM_SUMS, after, table,
    )


def add_halves(kept, arrived, after=()):
    two, rows, width = kept.shape
    half = rows // 2

    def body(kept_in, arrived, sent, kept):
        for i in range(2):
            total = kept_in[i] + arrived[i].astype(F32)
            kept[i] = total[:half]
            sent[i] = total[half:].astype(sent.dtype)

    shape = (two, half, width)
    return call(
        body, 1, [whole(kept), whole(arrived)],
        [((shape, BF), block_of(*shape)), ((shape, F32), block_of(*shape))],
        16, after, None, FLOPS,
    )


def activate(sums, arrived, after=()):
    two, rows, width = sums.shape

    def body(sums, arrived, out):
        gate, up = (sums[i] + arrived[i].astype(F32) for i in range(2))
        out[...] = (jax.nn.silu(gate) * up).astype(BF)

    return call(
        body, 1, [whole(sums), whole(arrived)],
        [(((rows, width), BF), block_of(rows, width))],
        12, after, None, FLOPS,
    )


def join(first, second, after=()):
    rows, width = first.shape

    def body(first, second, out):
        out[:rows] = first[...]
        out[rows:] = second[...]

    return call(
        body, 1, [whole(first), whole(second)],
        [(((2 * rows, width), BF), block_of(2 * rows, width))],
        12, after, None, FLOPS,
    )


def pack(table, selector, pairs):
    slots, rows = selector.shape
    half = sum(mine.shape[1] for mine, _ in pairs)

    def body(table, selector, *refs):
        out, start = refs[-1], 0
        for i, ref in enumerate(refs[:-1]):
            turn, count = i % 2, ref.shape[1]
            ordered = take(ref, table, 9 + 4 * turn, 4, rows // 4)
            value = dot(selector[...], ordered).astype(out.dtype)
            for side in range(2):
                @pl.when((table[0] ^ turn) == side)
                def _():
                    first = side * half + start
                    out[:, first : first + count] = value
            start += count * turn

    return call(
        body, 1, [whole(selector)] + [whole(v) for pair in pairs for v in pair],
        [(((slots, 2 * half), BF), block_of(slots, 2 * half))],
        20, (), table,
    )


def down(table, weight, pairs, after):
    depth, width = weight.shape
    rows = pairs[0].shape[0]
    half = depth // 2

    def body(table, weight, *refs):
        out = refs[-1]
        left = []
        for i, ref in enumerate(refs[:-1]):
            left.append(ref[...] if i % 2 == 0 else take(ref, table, 5, 4, rows // 4))
        for start in range(0, width, TILE):
            at = slice(start, start + TILE)
            total, offset = 0.0, 0
            for i, value in enumerate(left):
                side = table[0] if i % 2 == 0 else 1 - table[0]
                count = value.shape[1]
                first = pl.multiple_of(side * half + offset, 128)
                total = total + dot(value, weight[pl.ds(first, count), at])
                offset += count * (i % 2)
            out[:, at] = total

    return call(
        body, 1, [whole(weight)] + [whole(v) for v in pairs],
        [(((rows, width), F32), block_of(rows, width))],
        VM_DOWN, after, table,
    )


def low_rank(arrived, factor, after):
    groups, slots, width = arrived.shape
    ranks = factor.shape[0]

    def body(rows, factor, out):
        low = jnp.zeros((slots, ranks), F32)
        for h in range(groups):
            low = low + lax.dot_general(
                rows[h],
                factor[:, h * width : (h + 1) * width],
                (((1,), (1,)), ((), ())),
                preferred_element_type=F32,
            )
        out[...] = low

    return call(
        body, 1, [whole(arrived), whole(factor)],
        [(((slots, ranks), F32), block_of(slots, ranks))],
        VM_LOW, after,
    )


def up_project(low, factor, per_dev, pieces):
    slots, ranks = low.shape
    piece = factor.shape[1] // pieces

    def body(low, factor, out):
        total = low[...]
        row = lax.broadcasted_iota(jnp.int32, total.shape, 0) // (slots // per_dev)
        column = lax.broadcasted_iota(jnp.int32, total.shape, 1) // (ranks // per_dev)
        own = jnp.where(row == column, total, 0.0).astype(BF)
        for j in range(pieces):
            out[j] = dot(own, factor[:, j * piece : (j + 1) * piece]).astype(out.dtype)

    return call(
        body, 1, [whole(low), whole(factor)],
        [(((pieces, slots, piece), BF), block_of(pieces, slots, piece))],
        12,
    )


def halve(table, base):
    rows, columns = base.shape
    width = columns // 2
    count = 8
    block = rows // 2 // count
    half = block_of(rows // 2, width)

    def body(table, base, *outs):
        for stream in range(2):
            at = slice(stream * width, (stream + 1) * width)
            for ref, start in ((outs[2 * stream], count), (outs[2 * stream + 1], 0)):
                first = stream * 2 * count + start
                for p in range(count):
                    source = pl.multiple_of(table[first + p] * block, block)
                    ref[p * block : (p + 1) * block, :] = base[pl.ds(source, block), at].astype(
                        ref.dtype
                    )

    shape = (rows // 2, width)
    outs = [((shape, BF), half), ((shape, F32), half)] * 2
    return call(body, 1, [whole(base)], outs, 24, (), table)


def land_own(table, kept, arrived, landing, returned):
    half, width = kept[0].shape
    count = 8
    block = half // count

    def body(table, *refs):
        landing, returned = refs[4:6]
        for stream in range(2):
            first = (4 + 2 * stream) * count
            rows = dot(
                take(landing, table, first, count, block),
                returned[:, stream * width : (stream + 1) * width],
            )
            total = refs[stream][...] + refs[2 + stream][...].astype(F32)
            refs[6 + stream][...] = total + rows

    ins = [whole(v) for v in (*kept, *arrived, landing, returned)]
    outs = [(((half, width), F32), block_of(half, width))] * 2
    return call(body, 1, ins, outs, VM_LAND, (), table)


def land_other(table, kept, landings, returned):
    rows, width = kept[0].shape
    count = 8
    block, half = rows // count, rows // 2

    def body(table, *refs):
        for stream in range(2):
            first = (4 + 2 * stream) * count
            left = take(refs[2 + stream], table, first, count, block)
            total = refs[stream][...] + dot(left, refs[4 + stream][...])
            refs[6 + 2 * stream][...] = total[half:].astype(BF)
            refs[7 + 2 * stream][...] = total[:half]

    ins = [whole(v) for v in (*kept, *landings, *returned)]
    outs = [(((half, width), BF), block_of(half, width)), (((half, width), F32), block_of(half, width))]
    return call(body, 1, ins, outs * 2, VM_LAND, (), table)


def per_device(
    tokens, gate_weight, up_weight, down_weight, adapter_id, owner_slot, adapt_down, adapt_up
):
    x, z, y, c = (lax.axis_index(n) for n in ("x", "z", "y", "c"))
    row_count = tokens.shape[0]
    d_local = down_weight.shape[1]
    adapter_count = owner_slot.shape[0]
    per_dev, ff_count, rank = adapt_down.shape
    capacity = 2 * row_count // adapter_count
    slots = per_dev * capacity
    wid_axes, hid_axes = ("y", "c"), ("x", "z")
    wid_index, hid_index = y * 2 + c, x * 4 + z

    swap_perm = [(i, i ^ 1) for i in range(8)]
    first = (flip_a, flip_b)
    perm1 = [(v * 2 + k, first[k](v) * 2 + k) for v in range(4) for k in range(2)]
    perm2 = [(v * 2 + k, first[1 - k](v) * 2 + k) for v in range(4) for k in range(2)]

    gray_y = gray(y)
    low_y, high_y = gray_y & 1, gray_y >> 1
    four = jnp.arange(4, dtype=jnp.int32)

    def at_place(core):
        one, two = four >> 1, four & 1
        low = jnp.where(core == 0, one, two) ^ low_y
        high = jnp.where(core == 0, two, one) ^ high_y
        return low * 2 + high

    def place_of(core, blocks):
        low, high = (blocks >> 1) ^ low_y, (blocks & 1) ^ high_y
        return jnp.where(core == 0, low * 2 + high, high * 2 + low)

    home_blocks = at_place(c)
    table = jnp.concatenate([
        c[None], home_blocks, place_of(1 - c, home_blocks), place_of(c, four), place_of(1 - c, four)
    ])

    bits = jnp.stack([gray(x) >> 1, gray(x) & 1, gray(z) >> 1, gray(z) & 1])
    sixteen = jnp.arange(16, dtype=jnp.int32)
    land_tables, land_blocks = [], []
    for dims in STREAMS:
        found = []
        for d in range(4):
            shift = jnp.where(c == 0, 3 - dims[0].index(d), 3 - dims[1].index(d))
            found.append(((sixteen >> shift) & 1) ^ bits[d])
        at_x, at_z = gray(found[0] * 2 + found[1]), gray(found[2] * 2 + found[3])
        land_tables.append(place_of(c, at_x) * 4 + at_z)
        land_blocks.append(at_x * 4 + at_z)
    land_table = jnp.concatenate(land_tables + land_blocks)
    partners = []
    for dims in STREAMS:
        to = [
            jnp.where(
                (dims[k][0] < 2) == (v is x),
                flip_b(v) if dims[k][0] % 2 == 0 else flip_a(v),
                v,
            )
            for k in range(2)
            for v in (x, z)
        ]
        partners.append(jnp.where(c == 0, to[0] * 4 + to[1], to[2] * 4 + to[3]))
    place_index = jnp.stack([wid_index, hid_index, *partners]).astype(jnp.int32)
    (
        tokens, gate_weight, up_weight, table, land_table, place_index, adapter_id, owner_slot
    ) = lax.optimization_barrier((
        tokens, gate_weight, up_weight, table, land_table, place_index, adapter_id, owner_slot
    ))

    def selections(token):
        row_adapter = adapter_id[:, 0] + token[0, 0].astype(jnp.int32)
        adapter_range = jnp.arange(adapter_count, dtype=jnp.int32)
        row_slot = jnp.sum(
            jnp.where(row_adapter[:, None] == adapter_range[None, :], owner_slot[None, :], 0), axis=1
        )
        positions = jnp.arange(row_count, dtype=jnp.int32)
        earlier = (row_adapter[:, None] == row_adapter[None, :]) & (
            positions[None, :] < positions[:, None]
        )
        row_rank = jnp.sum(earlier.astype(jnp.int32), axis=1)
        shift = per_dev.bit_length() - 1
        owner_hid, owner_wid = row_slot >> (shift + 3), (row_slot >> shift) & 7
        place = (row_slot & (per_dev - 1)) * capacity + row_rank

        send_index = jnp.where(owner_wid == place_index[0:1], owner_hid * slots + place, -1)
        send_slots = jnp.arange(16 * slots, dtype=jnp.int32)[:, None]
        selector = (send_slots == send_index[None, :]).astype(BF)
        land_slots = jnp.arange(8 * slots, dtype=jnp.int32)[None, :]
        landings = []
        for i in range(3):
            index = jnp.where(owner_hid == place_index[1 + i : 2 + i], owner_wid * slots + place, -1)
            landings.append((index[:, None] == land_slots).astype(BF))
        return selector, landings

    down_factor = adapt_down.transpose(0, 2, 1).reshape(per_dev * rank, ff_count)
    up_factor = adapt_up.reshape(per_dev * rank, adapt_up.shape[2])

    swap, one, two = (
        lambda v, perm=perm: lax.ppermute(v, wid_axes, perm) for perm in (swap_perm, perm1, perm2)
    )
    far_tokens = swap(tokens)
    offsets = [sum(WIDTHS[:i]) for i in range(len(WIDTHS))]
    chunks = range(len(WIDTHS))
    sent, kept, hidden, theirs = ([None, None] for _ in range(4))
    weights = (gate_weight, up_weight)
    far, token = split_columns(table, *weights, offsets[0], WIDTHS[0], [])
    far = swap(far)
    token = [token, far_tokens]
    for i in chunks:
        own, token = own_sums(table, tokens, *weights, offsets[i], WIDTHS[i], token)
        this = far
        if i + 1 < len(WIDTHS):
            far, token = split_columns(
                table, *weights, offsets[i + 1], WIDTHS[i + 1], [token]
            )
            far = swap(far)
        sent[i], kept[i], token = add_sums(table, far_tokens, this, own, [token])
        token = [token]
    for i in chunks:
        sent[i], kept[i], token = add_halves(kept[i], one(sent[i]), token)
        token = [token]
    for i in chunks:
        hidden[i], token = activate(kept[i], two(sent[i]), token)
        token = [token]
        if i == 0:
            selector, landings = selections(token[0])
    for i in chunks:
        hidden[i], token = join(hidden[i], two(hidden[i]), token)
        token = [token]
    for i in chunks:
        hidden[i], token = join(hidden[i], one(hidden[i]), token)
        theirs[i] = swap(hidden[i])
        token = [token]
    pairs = [(hidden[i], theirs[i]) for i in chunks]
    packed, token = pack(table, selector, pairs)
    packed = packed.reshape(16, slots, packed.shape[1])
    arrived = lax.all_to_all(packed, hid_axes, split_axis=0, concat_axis=0, tiled=True)
    def cross(v, stream, step):
        perm = hid_perm([STREAMS[stream][k][step] for k in range(2)])
        return lax.ppermute(v, ("x", "z", "c"), perm)

    base, _ = down(table, down_weight, [v for pair in pairs for v in pair], [token])
    *ends, token = halve(land_table, base)
    kept = ends[1::2]
    sums = [cross(ends[2 * stream], stream, 0) for stream in range(2)]
    low, _ = low_rank(arrived, down_factor, [token])
    adapted, _ = up_project(low, up_factor, per_dev, 8)
    returned = lax.all_to_all(adapted, wid_axes, split_axis=0, concat_axis=0, tiled=True)
    returned = returned.reshape(8 * slots, d_local)
    width = d_local // 2
    others = [
        cross(returned[:, stream * width : (stream + 1) * width], stream, 0) for stream in range(2)
    ]
    *totals, _ = land_own(land_table, kept, sums, landings[0], returned)
    *ends, _ = land_other(land_table, totals, landings[1:], others)
    outs = []
    for stream in range(2):
        going, value = ends[2 * stream], ends[2 * stream + 1]
        for step in range(1, 4):
            if step > 1:
                half = value.shape[0] // 2
                going, value = value[half:].astype(STEP_TYPES[step]), value[:half]
            value = value + cross(going, stream, step).astype(F32)
        outs.append(value)
    return jnp.concatenate(outs, 1).astype(BF)


def solution(mesh):
    fine = Mesh(mesh.devices.reshape(4, 4, 4, 2), ("x", "z", "y", "c"))
    hid, wid = ("x", "z"), ("y", "c")
    return jax.shard_map(
        per_device,
        mesh=fine,
        in_specs=(
            P(None, wid),
            P(wid, hid),
            P(wid, hid),
            P(hid, wid),
            P(),
            P(),
            P(hid + wid, None, None),
            P(hid + wid, None, None),
        ),
        out_specs=P(hid, wid),
        check_vma=False,
    )
```

```python
import jax
import jax.numpy as jnp
from jax import lax
from jax.experimental import pallas as pl
from jax.experimental.pallas import tpu as pltpu
from jax.sharding import Mesh, PartitionSpec as P

BF = jnp.bfloat16
F32 = jnp.float32
TILE = 256
STEP_TYPES = (BF, BF, BF, BF)
VM_SPLIT, VM_OWN, VM_SUMS, VM_LOW, VM_DOWN, VM_LAND = 20, 20, 20, 16, 20, 16
WIDTHS = (512, 384)
FLOPS = 2 * 10**10
STREAMS = (((0, 1, 2, 3), (2, 3, 0, 1)), ((1, 0, 3, 2), (3, 2, 1, 0)))


def flip_a(v):
    return v ^ 1


def flip_b(v):
    return 3 - v


def gray(v):
    return v ^ (v >> 1)


def hid_perm(dims):
    pairs = []
    for x in range(4):
        for z in range(4):
            for k in range(2):
                move = flip_b if dims[k] % 2 == 0 else flip_a
                to = (move(x), z) if dims[k] < 2 else (x, move(z))
                pairs.append(((x * 4 + z) * 2 + k, (to[0] * 4 + to[1]) * 2 + k))
    return pairs


def dot(a, b):
    return jnp.dot(a, b, preferred_element_type=F32)


def take(ref, table, start, count, rows):
    return jnp.concatenate(
        [ref[pl.ds(pl.multiple_of(table[start + p] * rows, rows), rows), :] for p in range(count)], 0
    )


def call(body, grid, ins, outs, mib, after=(), table=None, flops=1):
    first = 0 if table is None else 1
    token_spec = pl.BlockSpec((8, 128), lambda *i: (0, 0))

    def kernel(*refs):
        used = refs[: first + len(ins)] + refs[first + len(ins) + len(after) :]
        used[first + len(ins) + len(outs)][...] = jnp.zeros((8, 128), F32)
        body(*used[: first + len(ins) + len(outs)], *used[first + len(ins) + len(outs) + 1 :])

    specs = [spec for _, spec in ins] + [pl.BlockSpec(memory_space=pl.ANY)] * len(after)
    args = [] if table is None else [table]
    args += [v for v, _ in ins] + list(after)
    return pl.pallas_call(
        kernel,
        out_shape=[jax.ShapeDtypeStruct(*o[0]) for o in outs]
        + [jax.ShapeDtypeStruct((8, 128), F32)],
        grid_spec=pltpu.PrefetchScalarGridSpec(
            num_scalar_prefetch=first,
            grid=(grid,),
            in_specs=specs,
            out_specs=[o[1] for o in outs] + [token_spec],
        ),
        compiler_params=pltpu.CompilerParams(
            vmem_limit_bytes=mib * 2**20, dimension_semantics=("arbitrary",)
        ),
        cost_estimate=pl.CostEstimate(flops=flops, bytes_accessed=1, transcendentals=0),
    )(*args)


def block_of(*shape):
    return pl.BlockSpec(shape, lambda *_: (0,) * len(shape))


def whole(v):
    return v, pl.BlockSpec(v.shape, lambda *_: (0,) * v.ndim)


def split_columns(table, weight, offset, count, after):
    depth, width = weight.shape[0], weight.shape[1] // 2

    def body(table, weight, out):
        out[...] = weight[:, offset : offset + count]

    block = pl.BlockSpec((depth, width), lambda j, t: (0, 1 - t[0]))
    return call(
        body, 1, [(weight, block)], [(((depth, count), BF), block_of(depth, count))],
        VM_SPLIT, after, table,
    )


def own_sums(table, tokens, weight, offset, count, after=()):
    rows, depth = tokens.shape
    width = weight.shape[1] // 2

    def body(table, tokens, weight, out):
        left = take(tokens, table, 1, 4, rows // 4)
        for start in range(0, count, TILE):
            stop = min(start + TILE, count)
            out[:, start:stop] = dot(left, weight[:, offset + start : offset + stop])

    block = pl.BlockSpec((depth, width), lambda j, t: (0, t[0]))
    return call(
        body, 1, [whole(tokens), (weight, block)],
        [(((rows, count), F32), block_of(rows, count))],
        VM_OWN, after, table,
    )


def add_sums(table, far_tokens, far, own, after=()):
    rows = far_tokens.shape[0]
    count = far[0].shape[1]
    half = rows // 2

    def body(table, far_tokens, *refs):
        sent, kept = refs[4:]
        left = take(far_tokens, table, 1, 4, rows // 4)
        for i in range(2):
            for start in range(0, count, TILE):
                at = slice(start, min(start + TILE, count))
                total = dot(left, refs[i][:, at]) + refs[2 + i][:, at]
                kept[i, :, at] = total[:half]
                sent[i, :, at] = total[half:].astype(sent.dtype)

    shape = (2, half, count)
    return call(
        body, 1, [whole(v) for v in (far_tokens, *far, *own)],
        [((shape, BF), block_of(*shape)), ((shape, F32), block_of(*shape))],
        VM_SUMS, after, table,
    )


def add_halves(kept, arrived, after=()):
    two, rows, width = kept.shape
    half = rows // 2

    def body(kept_in, arrived, sent, kept):
        for i in range(2):
            total = kept_in[i] + arrived[i].astype(F32)
            kept[i] = total[:half]
            sent[i] = total[half:].astype(sent.dtype)

    shape = (two, half, width)
    return call(
        body, 1, [whole(kept), whole(arrived)],
        [((shape, BF), block_of(*shape)), ((shape, F32), block_of(*shape))],
        16, after, None, FLOPS,
    )


def activate(sums, arrived, after=()):
    two, rows, width = sums.shape

    def body(sums, arrived, out):
        gate, up = (sums[i] + arrived[i].astype(F32) for i in range(2))
        out[...] = (jax.nn.silu(gate) * up).astype(BF)

    return call(
        body, 1, [whole(sums), whole(arrived)],
        [(((rows, width), BF), block_of(rows, width))],
        12, after, None, FLOPS,
    )


def join(first, second, after=()):
    rows, width = first.shape

    def body(first, second, out):
        out[:rows] = first[...]
        out[rows:] = second[...]

    return call(
        body, 1, [whole(first), whole(second)],
        [(((2 * rows, width), BF), block_of(2 * rows, width))],
        12, after, None, FLOPS,
    )


def pack(table, row_slot, row_rank, pairs, per_dev, capacity, after):
    rows = row_slot.shape[1]
    slots = 16 * per_dev * capacity
    half = sum(mine.shape[1] for mine, _ in pairs)
    shift = per_dev.bit_length() - 1

    def body(table, row_slot, row_rank, *refs):
        out, start = refs[-1], 0
        slot = row_slot[...]
        place = (slot & (per_dev - 1)) * capacity + row_rank[...]
        index = jnp.where(
            ((slot >> shift) & 7) == table[17],
            (slot >> (shift + 3)) * (per_dev * capacity) + place,
            -1,
        )
        at = lax.broadcasted_iota(jnp.int32, (slots, rows), 0)
        selector = jnp.where(at == index, 1.0, 0.0).astype(BF)
        for i, ref in enumerate(refs[:-1]):
            turn, count = i % 2, ref.shape[1]
            ordered = take(ref, table, 9 + 4 * turn, 4, rows // 4)
            value = dot(selector, ordered).astype(out.dtype)
            for side in range(2):
                @pl.when((table[0] ^ turn) == side)
                def _():
                    first = side * half + start
                    out[:, first : first + count] = value
            start += count * turn

    return call(
        body, 1, [whole(row_slot), whole(row_rank)] + [whole(v) for pair in pairs for v in pair],
        [(((slots, 2 * half), BF), block_of(slots, 2 * half))],
        20, after, table,
    )


def down(table, weight, pairs, after):
    depth, width = weight.shape
    rows = pairs[0].shape[0]
    half = depth // 2

    def body(table, weight, *refs):
        out = refs[-1]
        left = []
        for i, ref in enumerate(refs[:-1]):
            left.append(ref[...] if i % 2 == 0 else take(ref, table, 5, 4, rows // 4))
        for start in range(0, width, TILE):
            at = slice(start, start + TILE)
            total, offset = 0.0, 0
            for i, value in enumerate(left):
                side = table[0] if i % 2 == 0 else 1 - table[0]
                count = value.shape[1]
                first = pl.multiple_of(side * half + offset, 128)
                total = total + dot(value, weight[pl.ds(first, count), at])
                offset += count * (i % 2)
            out[:, at] = total

    return call(
        body, 1, [whole(weight)] + [whole(v) for v in pairs],
        [(((rows, width), F32), block_of(rows, width))],
        VM_DOWN, after, table,
    )


def low_rank(arrived, factor, after):
    groups, slots, width = arrived.shape
    ranks = factor.shape[0]

    def body(rows, factor, out):
        low = jnp.zeros((slots, ranks), F32)
        for h in range(groups):
            low = low + lax.dot_general(
                rows[h],
                factor[:, h * width : (h + 1) * width],
                (((1,), (1,)), ((), ())),
                preferred_element_type=F32,
            )
        out[...] = low

    return call(
        body, 1, [whole(arrived), whole(factor)],
        [(((slots, ranks), F32), block_of(slots, ranks))],
        VM_LOW, after,
    )


def up_project(low, factor, per_dev, pieces):
    slots, ranks = low.shape
    piece = factor.shape[1] // pieces

    def body(low, factor, out):
        total = low[...]
        row = lax.broadcasted_iota(jnp.int32, total.shape, 0) // (slots // per_dev)
        column = lax.broadcasted_iota(jnp.int32, total.shape, 1) // (ranks // per_dev)
        own = jnp.where(row == column, total, 0.0).astype(BF)
        for j in range(pieces):
            out[j] = dot(own, factor[:, j * piece : (j + 1) * piece]).astype(out.dtype)

    return call(
        body, 1, [whole(low), whole(factor)],
        [(((pieces, slots, piece), BF), block_of(pieces, slots, piece))],
        12,
    )


def halve(table, base):
    rows, columns = base.shape
    width = columns // 2
    count = 8
    block = rows // 2 // count
    half = block_of(rows // 2, width)

    def body(table, base, *outs):
        for stream in range(2):
            at = slice(stream * width, (stream + 1) * width)
            for ref, start in ((outs[2 * stream], count), (outs[2 * stream + 1], 0)):
                first = stream * 2 * count + start
                for p in range(count):
                    source = pl.multiple_of(table[first + p] * block, block)
                    ref[p * block : (p + 1) * block, :] = base[pl.ds(source, block), at].astype(
                        ref.dtype
                    )

    shape = (rows // 2, width)
    outs = [((shape, BF), half), ((shape, F32), half)] * 2
    return call(body, 1, [whole(base)], outs, 24, (), table)


def land_own(table, kept, arrived, landing, returned):
    half, width = kept[0].shape
    count = 8
    block = half // count

    def body(table, *refs):
        landing, returned = refs[4:6]
        for stream in range(2):
            first = (4 + 2 * stream) * count
            rows = dot(
                take(landing, table, first, count, block),
                returned[:, stream * width : (stream + 1) * width],
            )
            total = refs[stream][...] + refs[2 + stream][...].astype(F32)
            refs[6 + stream][...] = total + rows

    ins = [whole(v) for v in (*kept, *arrived, landing, returned)]
    outs = [(((half, width), F32), block_of(half, width))] * 2
    return call(body, 1, ins, outs, VM_LAND, (), table)


def land_other(table, kept, landings, returned):
    rows, width = kept[0].shape
    count = 8
    block, half = rows // count, rows // 2

    def body(table, *refs):
        for stream in range(2):
            first = (4 + 2 * stream) * count
            left = take(refs[2 + stream], table, first, count, block)
            total = refs[stream][...] + dot(left, refs[4 + stream][...])
            refs[6 + 2 * stream][...] = total[half:].astype(BF)
            refs[7 + 2 * stream][...] = total[:half]

    ins = [whole(v) for v in (*kept, *landings, *returned)]
    outs = [(((half, width), BF), block_of(half, width)), (((half, width), F32), block_of(half, width))]
    return call(body, 1, ins, outs * 2, VM_LAND, (), table)


def per_device(
    tokens, gate_weight, up_weight, down_weight, adapter_id, owner_slot, adapt_down, adapt_up
):
    x, z, y, c = (lax.axis_index(n) for n in ("x", "z", "y", "c"))
    row_count = tokens.shape[0]
    d_local = down_weight.shape[1]
    adapter_count = owner_slot.shape[0]
    per_dev, ff_count, rank = adapt_down.shape
    capacity = 2 * row_count // adapter_count
    slots = per_dev * capacity
    wid_axes, hid_axes = ("y", "c"), ("x", "z")
    wid_index, hid_index = y * 2 + c, x * 4 + z

    swap_perm = [(i, i ^ 1) for i in range(8)]
    first = (flip_a, flip_b)
    perm1 = [(v * 2 + k, first[k](v) * 2 + k) for v in range(4) for k in range(2)]
    perm2 = [(v * 2 + k, first[1 - k](v) * 2 + k) for v in range(4) for k in range(2)]

    gray_y = gray(y)
    low_y, high_y = gray_y & 1, gray_y >> 1
    four = jnp.arange(4, dtype=jnp.int32)

    def at_place(core):
        one, two = four >> 1, four & 1
        low = jnp.where(core == 0, one, two) ^ low_y
        high = jnp.where(core == 0, two, one) ^ high_y
        return low * 2 + high

    def place_of(core, blocks):
        low, high = (blocks >> 1) ^ low_y, (blocks & 1) ^ high_y
        return jnp.where(core == 0, low * 2 + high, high * 2 + low)

    home_blocks = at_place(c)
    table = jnp.concatenate([
        c[None], home_blocks, place_of(1 - c, home_blocks), place_of(c, four), place_of(1 - c, four),
        wid_index[None],
    ])

    bits = jnp.stack([gray(x) >> 1, gray(x) & 1, gray(z) >> 1, gray(z) & 1])
    sixteen = jnp.arange(16, dtype=jnp.int32)
    land_tables, land_blocks = [], []
    for dims in STREAMS:
        found = []
        for d in range(4):
            shift = jnp.where(c == 0, 3 - dims[0].index(d), 3 - dims[1].index(d))
            found.append(((sixteen >> shift) & 1) ^ bits[d])
        at_x, at_z = gray(found[0] * 2 + found[1]), gray(found[2] * 2 + found[3])
        land_tables.append(place_of(c, at_x) * 4 + at_z)
        land_blocks.append(at_x * 4 + at_z)
    land_table = jnp.concatenate(land_tables + land_blocks)
    partners = []
    for dims in STREAMS:
        to = [
            jnp.where(
                (dims[k][0] < 2) == (v is x),
                flip_b(v) if dims[k][0] % 2 == 0 else flip_a(v),
                v,
            )
            for k in range(2)
            for v in (x, z)
        ]
        partners.append(jnp.where(c == 0, to[0] * 4 + to[1], to[2] * 4 + to[3]))
    place_index = jnp.stack([wid_index, hid_index, *partners]).astype(jnp.int32)
    (
        tokens, gate_weight, up_weight, table, land_table, place_index, adapter_id, owner_slot
    ) = lax.optimization_barrier((
        tokens, gate_weight, up_weight, table, land_table, place_index, adapter_id, owner_slot
    ))

    def selections(token):
        row_adapter = adapter_id[:, 0] + token[0, 0].astype(jnp.int32)
        adapter_range = jnp.arange(adapter_count, dtype=jnp.int32)
        row_slot = jnp.sum(
            jnp.where(row_adapter[:, None] == adapter_range[None, :], owner_slot[None, :], 0), axis=1
        )
        positions = jnp.arange(row_count, dtype=jnp.int32)
        earlier = (row_adapter[:, None] == row_adapter[None, :]) & (
            positions[None, :] < positions[:, None]
        )
        row_rank = jnp.sum(earlier.astype(jnp.int32), axis=1)
        return row_slot, row_rank

    def landing_index(row_slot, row_rank):
        shift = per_dev.bit_length() - 1
        owner_hid, owner_wid = row_slot >> (shift + 3), (row_slot >> shift) & 7
        place = (row_slot & (per_dev - 1)) * capacity + row_rank
        return [
            jnp.where(owner_hid == place_index[1 + i : 2 + i], owner_wid * slots + place, -1)
            for i in range(3)
        ]

    down_factor = adapt_down.transpose(0, 2, 1).reshape(per_dev * rank, ff_count)
    up_factor = adapt_up.reshape(per_dev * rank, adapt_up.shape[2])

    swap, one, two = (
        lambda v, perm=perm: lax.ppermute(v, wid_axes, perm) for perm in (swap_perm, perm1, perm2)
    )
    far_tokens = swap(tokens)
    offsets = [sum(WIDTHS[:i]) for i in range(len(WIDTHS))]
    chunks = range(len(WIDTHS))
    sent, kept, hidden, theirs = ([None, None] for _ in range(4))
    weights = (gate_weight, up_weight)
    token = []
    for i in chunks:
        far, own = [None, None], [None, None]
        for k in range(2):
            far[k], token = split_columns(table, weights[k], offsets[i], WIDTHS[i], token)
            far[k] = swap(far[k])
            own[k], token = own_sums(table, tokens, weights[k], offsets[i], WIDTHS[i], [token])
            token = [token]
            if i == 0 and k == 0:
                token.append(far_tokens)
        sent[i], kept[i], token = add_sums(table, far_tokens, far, own, token)
        token = [token]
    for i in chunks:
        sent[i], kept[i], token = add_halves(kept[i], one(sent[i]), token)
        token = [token]
    for i in chunks:
        hidden[i], token = activate(kept[i], two(sent[i]), token)
        token = [token]
        if i == 0:
            row_slot, row_rank = selections(token[0])
    for i in chunks:
        hidden[i], token = join(hidden[i], two(hidden[i]), token)
        token = [token]
    for i in chunks:
        hidden[i], token = join(hidden[i], one(hidden[i]), token)
        theirs[i] = swap(hidden[i])
        token = [token]
    pairs = [(hidden[i], theirs[i]) for i in chunks]
    indices = landing_index(row_slot, row_rank)
    packed, token = pack(
        table, row_slot[None, :], row_rank[None, :], pairs, per_dev, capacity, indices
    )
    packed = packed.reshape(16, slots, packed.shape[1])
    arrived = lax.all_to_all(packed, hid_axes, split_axis=0, concat_axis=0, tiled=True)
    def cross(v, stream, step):
        perm = hid_perm([STREAMS[stream][k][step] for k in range(2)])
        return lax.ppermute(v, ("x", "z", "c"), perm)

    base, _ = down(table, down_weight, [v for pair in pairs for v in pair], [token])
    *ends, token = halve(land_table, base)
    kept = ends[1::2]
    sums = [cross(ends[2 * stream], stream, 0) for stream in range(2)]
    low, _ = low_rank(arrived, down_factor, [token])
    adapted, _ = up_project(low, up_factor, per_dev, 8)
    land_slots = jnp.arange(8 * slots, dtype=jnp.int32)[None, :]
    landings = [(index[:, None] == land_slots).astype(BF) for index in indices]
    returned = lax.all_to_all(adapted, wid_axes, split_axis=0, concat_axis=0, tiled=True)
    returned = returned.reshape(8 * slots, d_local)
    width = d_local // 2
    others = [
        cross(returned[:, stream * width : (stream + 1) * width], stream, 0) for stream in range(2)
    ]
    *totals, _ = land_own(land_table, kept, sums, landings[0], returned)
    *ends, _ = land_other(land_table, totals, landings[1:], others)
    outs = []
    for stream in range(2):
        going, value = ends[2 * stream], ends[2 * stream + 1]
        for step in range(1, 4):
            if step > 1:
                half = value.shape[0] // 2
                going, value = value[half:].astype(STEP_TYPES[step]), value[:half]
            value = value + cross(going, stream, step).astype(F32)
        outs.append(value)
    return jnp.concatenate(outs, 1).astype(BF)


def solution(mesh):
    fine = Mesh(mesh.devices.reshape(4, 4, 4, 2), ("x", "z", "y", "c"))
    hid, wid = ("x", "z"), ("y", "c")
    return jax.shard_map(
        per_device,
        mesh=fine,
        in_specs=(
            P(None, wid),
            P(wid, hid),
            P(wid, hid),
            P(hid, wid),
            P(),
            P(),
            P(hid + wid, None, None),
            P(hid + wid, None, None),
        ),
        out_specs=P(hid, wid),
        check_vma=False,
    )
```
